32 devices in a mesh: shard: 8 (over y, x, core), tensor: 4 (over z).
Axes of the slice: x: 2, y: 2, z: 4, core: 2. Of those that a mesh axis runs over, the one named last changes fastest.
Arguments:
- grads: bfloat16 [4096, 2048], P('shard', 'tensor'), may hold values from -120 to 120
- assignment: int32 [4, 8], P('tensor'), may hold values from 0 to 7, as said below
- moment: float32 [8, 2048, 512], P('shard', 'tensor'), may hold values from -6 to 6
- second: float32 [8, 2048, 512], P('shard', 'tensor'), may hold values from 0.2 to 2
- left_stats: float32 [8, 2048, 512], P('shard', 'tensor'), may hold values from -0.02 to 3.1, as said below
- right_stats: float32 [8, 2048, 512], P('shard', 'tensor'), may hold values from -0.02 to 3.1, as said below
- left_basis: float32 [8, 2048, 512], P('shard', 'tensor'), may hold values from -0.25 to 0.25
- right_basis: float32 [8, 2048, 512], P('shard', 'tensor'), may hold values from -0.25 to 0.25
Outputs:
- update: bfloat16 [4096, 2048], P('shard', 'tensor')
- new_moment: float32 [8, 2048, 512], P('shard', 'tensor')
- new_second: float32 [8, 2048, 512], P('shard', 'tensor')
- new_left_stats: float32 [8, 2048, 512], P('shard', 'tensor')
- new_right_stats: float32 [8, 2048, 512], P('shard', 'tensor')
- new_left_basis: float32 [8, 2048, 512], P('shard', 'tensor')
- new_right_basis: float32 [8, 2048, 512], P('shard', 'tensor')
The draws below stay inside these ranges and needn't reach their ends.
Inputs may be any that keep to these rules, and one draw needn't show every extreme that they name: `assignment`: within each block column the slots are distinct; slot a lies on index a // 1 of shard as its slot a % 1; in every block column some index of shard holds 1 block. `left_stats`: statistics carried from earlier steps. `right_stats`: statistics carried from earlier steps.
All inputs are finite; a program needn't handle non-finite values.
Results may differ from the reference program's by a relative error of at most 0.0004.
Values may be sent and summed in bfloat16 or wider, within the bound.
A program may use at most 128 MiB of HBM per device.

```python
import math
import jax
import jax.numpy as jnp
from jax import lax

D = 2048
BLOCK = 512
SLOTS = 1
NS_ITERS = 2
ROWS = 4096
OWNER_SLOTS = 8


def draw_grads(key, part):
    key_base = jax.random.fold_in(key, 3)
    key_noise, key_rows, key_columns = jax.random.split(key_base, 3)
    row_position = jnp.arange(ROWS, dtype=jnp.float32) / ROWS
    row_scale = 10.0 ** (jax.random.uniform(key_rows, (ROWS,), jnp.float32) - 0.5)
    column_scale = 10.0 ** (jax.random.uniform(key_columns, (D,), jnp.float32) - 0.5)
    entries = jnp.clip(jax.random.normal(key_noise, (ROWS, D), jnp.float32), -4.0, 4.0)
    row_trend = jnp.exp(0.5 * math.log(3.0) * row_position)
    scaled = entries * (row_trend * row_scale)[:, None] * column_scale[None, :]
    return scaled.astype(jnp.bfloat16)


def draw_assignment(key, part):
    key_base = jax.random.fold_in(key, 5)
    owner_count = OWNER_SLOTS // SLOTS
    column_count = D // BLOCK

    def one_column(column_key):
        key_scores, key_chosen, key_order = jax.random.split(column_key, 3)
        scores = jax.random.permutation(key_scores, OWNER_SLOTS).astype(jnp.int32)
        chosen = jax.random.randint(key_chosen, (), 0, owner_count, dtype=jnp.int32)
        scores = scores.at[OWNER_SLOTS - 1].set(-1 - SLOTS)
        forced = chosen * SLOTS + jnp.arange(SLOTS, dtype=jnp.int32)
        scores = scores.at[forced].set(jnp.arange(SLOTS, dtype=jnp.int32) - SLOTS)
        ranked = jnp.argsort(scores, stable=True)[:owner_count].astype(jnp.int32)
        shuffle = jax.random.permutation(key_order, owner_count)
        return ranked[shuffle]
    column_keys = jax.random.split(key_base, column_count)
    return jax.vmap(one_column)(column_keys).astype(jnp.int32)


def statistics_draw(key):
    column_count = D // BLOCK
    key_noise, key_diagonal = jax.random.split(key)
    shape = (OWNER_SLOTS, column_count, BLOCK, BLOCK)
    noise = jnp.clip(jax.random.normal(key_noise, shape, jnp.float32), -4.0, 4.0) * 0.002
    diagonal = jnp.exp(jax.random.uniform(key_diagonal, (OWNER_SLOTS, column_count, BLOCK), jnp.float32, math.log(0.2), math.log(2.0)))
    symmetric = 0.5 * (noise + jnp.swapaxes(noise, 2, 3))
    identity_mask = (jnp.arange(BLOCK)[:, None] == jnp.arange(BLOCK)[None, :]).astype(jnp.float32)
    result = symmetric + identity_mask * diagonal[:, :, :, None]
    return result.reshape(OWNER_SLOTS, D, BLOCK).astype(jnp.float32)


def draw_left_stats(key, part):
    return statistics_draw(jax.random.fold_in(key, 11))


def draw_right_stats(key, part):
    return statistics_draw(jax.random.fold_in(key, 23))


def block_levels(key, dims, pieces, low, largest):
    def one(axis_at, blocks):
        draws = jax.random.uniform(jax.random.fold_in(jax.random.fold_in(key, 6), axis_at), (blocks,), jnp.float32, low / len(pieces), largest / len(pieces))
        return jnp.repeat(jnp.exp(draws), dims[axis_at] // blocks).reshape((-1,) + (1,) * (len(dims) - axis_at - 1))

    factor_of = one(*pieces[0])
    for cut in pieces[1:]:
        factor_of = factor_of * one(*cut)
    return factor_of


def normal_values(key, extent, scale, most, cuts=(), held_as=jnp.bfloat16):
    values = scale * jax.random.normal(key, extent, jnp.float32)
    if cuts:
        values = values * block_levels(key, extent, cuts, -0.22, 0.18)
    return jnp.clip(values, -most, most).astype(held_as)


def setup_inputs(seed: int = 0) -> dict:
    streams_of = jax.random.split(jax.random.key(seed), 9)
    grads = draw_grads(jax.random.fold_in(streams_of[8], 71), 0)
    assignment = draw_assignment(jax.random.fold_in(streams_of[8], 71), 0)
    moment = normal_values(streams_of[2], (OWNER_SLOTS, D, BLOCK), 1.0, 6.0, ((0, 8), (1, 4)), jnp.float32)
    second = jnp.clip(jnp.exp(math.log(2.0) - 2.3025851 * jax.random.uniform(streams_of[3], (OWNER_SLOTS, D, BLOCK), jnp.float32) ** block_levels(streams_of[3], (OWNER_SLOTS, D, BLOCK), ((0, 8), (1, 4)), -0.2, 0.2)), 0.2, 2.0)
    left_stats = draw_left_stats(jax.random.fold_in(streams_of[8], 71), 0)
    right_stats = draw_right_stats(jax.random.fold_in(streams_of[8], 71), 0)
    left_basis = normal_values(streams_of[6], (OWNER_SLOTS, D, BLOCK), BLOCK ** -0.5, 0.25, ((0, 8), (1, 4)), jnp.float32)
    right_basis = normal_values(streams_of[7], (OWNER_SLOTS, D, BLOCK), BLOCK ** -0.5, 0.25, ((0, 8), (1, 4)), jnp.float32)
    return {"grads": grads, "assignment": assignment, "moment": moment, "second": second, "left_stats": left_stats, "right_stats": right_stats, "left_basis": left_basis, "right_basis": right_basis}


BETA_MOMENT = 0.9
BETA_SECOND = 0.9
BETA_STATS = 0.9
ADAM_EPSILON = 1e-08
CLIP_RMS = 1.0
QUINTIC_A = 3.4445
QUINTIC_B = -4.775
QUINTIC_C = 2.0315

def highest_dot(left_side, right_side):
    return jnp.dot(left_side, right_side, precision=lax.Precision.HIGHEST, preferred_element_type=jnp.float32)

def orthonormal(product):
    iterate = product * lax.rsqrt(jnp.sum(product * product) + 1e-12)
    for sweep in range(NS_ITERS):
        gram_matrix = highest_dot(iterate.T, iterate)
        polynomial = QUINTIC_B * gram_matrix + QUINTIC_C * highest_dot(gram_matrix, gram_matrix)
        iterate = QUINTIC_A * iterate + highest_dot(iterate, polynomial)
    return iterate

def tile_update(grad_tile, factor, moment, second, left_old, right_old, left_rot, right_rot):
    block_size = grad_tile.shape[0]
    grad_float = grad_tile.astype(jnp.float32) * factor
    scale_stats = (1.0 - BETA_STATS) * factor * factor / block_size
    left_new = BETA_STATS * left_old + scale_stats * jnp.dot(grad_tile, grad_tile.T, preferred_element_type=jnp.float32)
    right_new = BETA_STATS * right_old + scale_stats * jnp.dot(grad_tile.T, grad_tile, preferred_element_type=jnp.float32)
    moment_new = BETA_MOMENT * moment + (1.0 - BETA_MOMENT) * grad_float
    rotated = highest_dot(highest_dot(left_rot.T, grad_float), right_rot)
    rotated_moment = highest_dot(highest_dot(left_rot.T, moment_new), right_rot)
    second_new = BETA_SECOND * second + (1.0 - BETA_SECOND) * rotated * rotated
    direction = rotated_moment / (jnp.sqrt(second_new) + ADAM_EPSILON)
    update = highest_dot(highest_dot(left_rot, direction), right_rot.T).astype(jnp.bfloat16)
    left_basis_new = orthonormal(highest_dot(left_old, left_rot))
    right_basis_new = orthonormal(highest_dot(right_old, right_rot))
    return (update, moment_new, second_new, left_new, right_new, left_basis_new, right_basis_new)

def reference(grads, assignment, moment, second, left_stats, right_stats, left_basis, right_basis):
    grad_float = grads.astype(jnp.float32)
    energy = jnp.sum(grad_float * grad_float)
    factor = jnp.minimum(1.0, CLIP_RMS / jnp.sqrt(energy / (ROWS * D) + 1e-12))
    block_rows = ROWS // BLOCK
    column_count = D // BLOCK
    updates = jnp.zeros((ROWS, D), jnp.bfloat16)
    zero_index = jnp.zeros((), jnp.int32)

    def visit(carry, flat_index):
        updates_now = carry[0]
        states = carry[1:]
        column = (flat_index // block_rows).astype(jnp.int32)
        tile_row = (flat_index % block_rows).astype(jnp.int32)
        slot_id = assignment[column, tile_row].astype(jnp.int32)
        row_start = (tile_row * BLOCK).astype(jnp.int32)
        column_start = (column * BLOCK).astype(jnp.int32)
        grad_tile = lax.dynamic_slice(grads, (row_start, column_start), (BLOCK, BLOCK))
        olds = tuple((lax.dynamic_slice(state, (slot_id, column_start, zero_index), (1, BLOCK, BLOCK))[0] for state in states))
        results = tile_update(grad_tile, factor, *olds)
        updates_now = lax.dynamic_update_slice(updates_now, results[0], (row_start, column_start))
        states = tuple((lax.dynamic_update_slice(state, fresh[None], (slot_id, column_start, zero_index)) for state, fresh in zip(states, results[1:])))
        return ((updates_now,) + states, None)
    start = (updates, moment, second, left_stats, right_stats, left_basis, right_basis)
    final, unused = lax.scan(visit, start, jnp.arange(block_rows * column_count, dtype=jnp.int32))
    return (final[0], final[1], final[2], final[3], final[4], final[5], final[6])
```

```python
import functools

import jax
import jax.numpy as jnp
from jax import lax
from jax.experimental import pallas as pl
from jax.experimental.pallas import tpu as pltpu
from jax.sharding import PartitionSpec as P

NS_ITERS = 2
BETA_MOMENT = 0.9
BETA_SECOND = 0.9
BETA_STATS = 0.9
ADAM_EPSILON = 1e-08
CLIP_RMS = 1.0
QUINTIC_A = 3.4445
QUINTIC_B = -4.775
QUINTIC_C = 2.0315
MESH = pl.DeviceIdType.MESH
F32 = jnp.float32
BF16 = jnp.bfloat16


def nn(a, b):
    return jnp.dot(a, b, preferred_element_type=F32)


def nt(a, b):
    return lax.dot_general(a, b, (((1,), (1,)), ((), ())), preferred_element_type=F32)


def split(x):
    high = x.astype(BF16)
    return high, (x - high.astype(F32)).astype(BF16)


def put(ref, x, order, axis):
    n = x.shape[0]
    parts = split(x)
    for place, part in enumerate(order):
        if axis:
            ref[:, place * n : (place + 1) * n] = parts[part]
        else:
            ref[place * n : (place + 1) * n, :] = parts[part]


LEFT = (0, 1, 0)
RIGHT = (0, 0, 1)


class Route:
    def __init__(self, nx, ny, half, src, first, out, second, sems, wanted):
        self.nx, self.ny, self.half, self.src = nx, ny, half, src
        self.first, self.out, self.second = first, out, second
        self.send1, self.recv1, self.send2, self.recv2 = sems
        self.wanted = wanted
        me = lax.axis_index("shard")
        self.me = me
        self.core = me % 2
        self.x = (me // 2) % nx
        self.y = me // (2 * nx)
        self.lines = ((0, nx, self.x, ny, self.y), (1, ny, self.y, nx, self.x))

    def device(self, kind, along, across, core):
        if kind == 0:
            return {"shard": (across * self.nx + along) * 2 + core}
        return {"shard": (along * self.nx + across) * 2 + core}

    def piece(self, kind):
        return self.src.at[pl.ds(kind * self.half, self.half), :]

    def copy1(self, kind, src, entry, slot, device):
        return pltpu.make_async_remote_copy(
            src_ref=src,
            dst_ref=self.first[kind].at[entry],
            send_sem=self.send1.at[kind, slot],
            recv_sem=self.recv1.at[kind, entry],
            device_id=device,
            device_id_type=MESH,
        )

    def own(self, kind, step):
        _, size, pos, _, other = self.lines[kind]
        to = (pos + step) % size
        return self.copy1(
            kind, self.piece(kind), pos * 2 + self.core, step, self.device(kind, to, other, self.core)
        )

    def relay(self, kind, step):
        _, size, pos, _, other = self.lines[kind]
        if step == 0:
            src = self.piece(kind)
            entry = pos * 2 + self.core
        else:
            entry = ((pos - step) % size) * 2 + self.core
            src = self.first[kind].at[entry]
        return self.copy1(
            kind, src, entry, size + step, self.device(kind, pos, other, 1 - self.core)
        )

    def start(self):
        for kind in range(2):
            for step in range(1, self.lines[kind][1]):
                self.own(kind, step).start()
        for kind in range(2):
            self.relay(kind, 0).start()

    def keep(self):
        for kind in range(2):
            _, size, pos, _, other = self.lines[kind]
            self.first[kind][pos * 2 + self.core] = self.piece(kind)[...]

    def pass_on(self, kind):
        _, size, pos, _, other = self.lines[kind]
        for step in range(1, size):
            entry = ((pos - step) % size) * 2 + self.core
            self.copy1(kind, self.piece(kind), entry, 0, self.device(kind, pos, other, self.core)).wait_recv()
            self.relay(kind, step).start()

    def copy2(self, kind, step):
        _, size, pos, across, other = self.lines[kind]
        to = (other + step) % across
        return pltpu.make_async_remote_copy(
            src_ref=self.out[kind].at[step],
            dst_ref=self.second[kind].at[other],
            send_sem=self.send2.at[kind, step],
            recv_sem=self.recv2.at[kind, other],
            device_id=self.device(kind, pos, to, self.core),
            device_id_type=MESH,
        )

    def entry_of(self, kind, block):
        if kind == 0:
            return block % (2 * self.nx)
        return (block // (2 * self.nx)) * 2 + block % 2

    def choose(self, kind):
        _, size, pos, across, other = self.lines[kind]
        for step in range(size):
            entry = ((pos - step) % size) * 2 + 1 - self.core
            self.copy1(kind, self.piece(kind), entry, 0, self.device(kind, pos, other, self.core)).wait_recv()
        for step in range(1, across):
            to = (other + step) % across
            block = self.wanted(self.device(kind, pos, to, self.core)["shard"])
            self.out[kind][step] = self.first[kind][self.entry_of(kind, block)]
            self.copy2(kind, step).start()
        block = self.wanted(self.me)
        self.second[kind][other] = self.first[kind][self.entry_of(kind, block)]

    def take(self, kind):
        _, size, pos, across, other = self.lines[kind]
        for step in range(1, across):
            frm = (other - step) % across
            pltpu.make_async_remote_copy(
                src_ref=self.out[kind].at[step],
                dst_ref=self.second[kind].at[frm],
                send_sem=self.send2.at[kind, step],
                recv_sem=self.recv2.at[kind, frm],
                device_id=self.device(kind, pos, (other + step) % across, self.core),
                device_id_type=MESH,
            ).wait_recv()
        block = self.wanted(self.me)
        index = block // (2 * self.nx) if kind == 0 else (block // 2) % self.nx
        return self.second[kind][index]

    def finish(self):
        for kind in range(2):
            _, size, pos, across, other = self.lines[kind]
            for step in range(1, size):
                self.own(kind, step).wait_send()
            for step in range(size):
                self.relay(kind, step).wait_send()
            for step in range(1, across):
                self.copy2(kind, step).wait_send()


def kernel(nx, ny, nz, entries, *refs):
    (grads, table, moment, second, left, right, pbasis, qbasis) = refs[:8]
    (o_up, o_m, o_v, o_l, o_r, o_p, o_q) = refs[8:15]
    (
        g_v, m_v, v_v, l_v, r_v, p_v, q_v,
        gg, up, mrot, y_s, a_s,
        ptl, plh, qr, qnt, qtl, x1, x2, x3,
        fx, fy, gx, gy, sx, sy,
        rfx, rfy, rgx, rgy, rsx, rsy,
        es, ebuf, ezs, ez,
        in_sem, out_sem, s1, r1, s2, r2, t1, u1, t2, u2, esend, erecv, zsend, zrecv,
    ) = refs[15:]
    n = g_v.shape[0]
    half = n // 2
    shards = nx * ny * 2
    me = lax.axis_index("shard")
    mz = lax.axis_index("tensor")

    order = ((grads, g_v), (pbasis, p_v), (left, l_v), (moment, m_v), (qbasis, q_v), (second, v_v), (right, r_v))
    loads = [pltpu.make_async_copy(a, b, in_sem.at[i]) for i, (a, b) in enumerate(order)]
    for load in loads:
        load.start()

    barrier = pltpu.get_barrier_semaphore()
    for step in range(1, shards):
        pl.semaphore_signal(barrier, inc=1, device_id={"shard": (me + step) % shards}, device_id_type=MESH)
    for step in range(1, nz):
        pl.semaphore_signal(barrier, inc=1, device_id={"tensor": (mz + step) % nz}, device_id_type=MESH)

    def row_of_slot(device):
        found = jnp.int32(0)
        for k in range(shards):
            found = jnp.where(table[0, k] == device, k, found)
        return found

    used = jnp.bool_(False)
    for k in range(shards):
        used = used | (table[0, k] == me)

    gather = Route(nx, ny, half, g_v, (fx, fy), (gx, gy), (sx, sy), (s1, r1, s2, r2), row_of_slot)
    give = Route(
        nx, ny, half, up, (rfx, rfy), (rgx, rgy), (rsx, rsy), (t1, u1, t2, u2), lambda d: table[0, d]
    )

    loads[0].wait()
    pl.semaphore_wait(barrier, shards - 1 + nz - 1)
    gather.start()

    gf = g_v[...].astype(F32)
    part = jnp.sum((gf * gf).reshape(n // 8, 8, n), axis=0)
    total = part[:, :128]
    for k in range(1, n // 128):
        total = total + part[:, k * 128 : (k + 1) * 128]
    es[...] = total
    ebuf[me] = total

    def energy_copy(step, src_of):
        return pltpu.make_async_remote_copy(
            src_ref=es,
            dst_ref=ebuf.at[src_of],
            send_sem=esend.at[step],
            recv_sem=erecv.at[src_of],
            device_id={"shard": (me + step) % shards},
            device_id_type=MESH,
        )

    def energy_copy_z(step, src_of):
        return pltpu.make_async_remote_copy(
            src_ref=ezs,
            dst_ref=ez.at[src_of],
            send_sem=zsend.at[step],
            recv_sem=zrecv.at[src_of],
            device_id={"tensor": (mz + step) % nz},
            device_id_type=MESH,
        )

    for step in range(1, shards):
        energy_copy(step, me).start()
    gather.keep()

    stores = []

    def store(src, dst):
        copy = pltpu.make_async_copy(src, dst, out_sem.at[len(stores)])
        copy.start()
        stores.append(copy)

    def orth(basis, out, points):
        y = y_s[...]
        y = y * lax.rsqrt(jnp.sum(y * y) + 1e-12)
        for sweep in range(NS_ITERS):
            y_s[...] = y
            put(x3, y, LEFT, 1)
            put(x2, y, RIGHT, 1)
            put(x1, y, RIGHT, 0)
            a = nt(x3[...], x2[...])
            a_s[...] = a
            points.pop(0)()
            put(x3, a, LEFT, 1)
            put(x2, a, RIGHT, 1)
            b = nt(x3[...], x2[...])
            put(x3, QUINTIC_B * a_s[...] + QUINTIC_C * b, LEFT, 1)
            points.pop(0)()
            y = QUINTIC_A * y_s[...] + nn(x3[...], x1[...])
        basis[...] = jnp.where(used, y.T, basis[...])
        store(basis, out)

    def nothing():
        pass

    loads[1].wait()
    p = p_v[...]
    put(plh, p, LEFT, 1)
    put(ptl, p.T, LEFT, 1)
    loads[2].wait()
    put(x2, l_v[...], RIGHT, 1)
    y_s[...] = nt(ptl[...], x2[...])

    def energy_z():
        for step in range(1, shards):
            energy_copy(step, (me - step) % shards).wait_recv()
        total = jnp.sum(ebuf[...], axis=0)
        ezs[...] = total
        ez[mz] = total
        for step in range(1, nz):
            energy_copy_z(step, mz).start()

    def passing():
        gather.pass_on(0)
        gather.pass_on(1)

    def choosing():
        gather.choose(0)
        gather.choose(1)

    orth(p_v, o_p, [energy_z, nothing, passing, choosing])

    loads[4].wait()
    q = q_v[...]
    put(qr, q, RIGHT, 0)
    put(qnt, q, RIGHT, 1)
    put(qtl, q.T, LEFT, 1)
    loads[3].wait()
    put(x1, m_v[...], RIGHT, 0)
    put(x3, nn(ptl[...], x1[...]), LEFT, 1)
    mrot[...] = nn(x3[...], qr[...])

    for step in range(1, nz):
        energy_copy_z(step, (mz - step) % nz).wait_recv()
    energy = jnp.sum(jnp.sum(ez[...], axis=0), keepdims=True)
    factor = jnp.minimum(1.0, CLIP_RMS / jnp.sqrt(energy / entries + 1e-12))

    gg[0:half, :] = gather.take(0)
    gg[half:n, :] = gather.take(1)
    g = gg[...]
    x1[0:n, :] = g
    x1[n : 2 * n, :] = g
    put(x3, nn(ptl[:, 0 : 2 * n], x1[0 : 2 * n, :]), LEFT, 1)
    rotated = factor * nn(x3[...], qr[...])
    loads[5].wait()
    v_new = BETA_SECOND * v_v[...] + (1.0 - BETA_SECOND) * rotated * rotated
    direction = (BETA_MOMENT * mrot[...] + (1.0 - BETA_MOMENT) * rotated) / (jnp.sqrt(v_new) + ADAM_EPSILON)
    v_v[...] = jnp.where(used, v_new, v_v[...])
    put(x1, direction, RIGHT, 0)
    store(v_v, o_v)
    put(x3, nn(plh[...], x1[...]), LEFT, 1)
    up[...] = nt(x3[...], qnt[...]).astype(BF16)
    give.start()
    give.keep()

    keep_m = jnp.where(used, BETA_MOMENT, 1.0)
    add_m = jnp.where(used, (1.0 - BETA_MOMENT) * factor, 0.0)
    keep_s = jnp.where(used, BETA_STATS, 1.0)
    add_s = jnp.where(used, (1.0 - BETA_STATS) * factor * factor / n, 0.0)
    m_v[...] = keep_m * m_v[...] + add_m * gg[...].astype(F32)
    store(m_v, o_m)
    loads[6].wait()
    put(x2, r_v[...], RIGHT, 1)
    y_s[...] = nt(qtl[...], x2[...])
    g = gg[...]
    l_v[...] = keep_s * l_v[...] + add_s * nt(g, g)
    store(l_v, o_l)
    gt = g.T
    r_v[...] = keep_s * r_v[...] + add_s * nt(gt, gt)
    store(r_v, o_r)

    def giving():
        give.pass_on(0)
        give.pass_on(1)

    def picking():
        give.choose(0)
        give.choose(1)

    orth(q_v, o_q, [nothing, nothing, giving, picking])

    gather.finish()
    for step in range(1, shards):
        energy_copy(step, me).wait_send()
    for step in range(1, nz):
        energy_copy_z(step, mz).wait_send()
    gg[0:half, :] = give.take(0)
    gg[half:n, :] = give.take(1)
    store(gg, o_up)
    give.finish()
    for copy in stores:
        copy.wait()


def shards_program(nx, ny, nz, entries, grads, assignment, *states):
    n = grads.shape[1]
    half = n // 2
    states = [s.reshape(n, n) for s in states]
    square = lambda dtype: pltpu.VMEM((n, n), dtype)
    wide = pltpu.VMEM((n, 3 * n), BF16)
    tall = pltpu.VMEM((3 * n, n), BF16)
    pieces = lambda count: pltpu.VMEM((count, half, n), BF16)
    longest = max(nx, ny)
    dma = lambda *shape: pltpu.SemaphoreType.DMA(shape)
    route = [pieces(2 * nx), pieces(2 * ny), pieces(ny), pieces(nx), pieces(ny), pieces(nx)]
    route_sems = [dma(2, 2 * longest), dma(2, 2 * longest), dma(2, longest), dma(2, longest)]
    shards = nx * ny * 2
    scratch = (
        [square(BF16)] + [square(F32)] * 6
        + [square(BF16), square(BF16), square(F32), square(F32), square(F32)]
        + [wide, wide, tall, wide, wide, tall, wide, wide]
        + route + route
        + [pltpu.VMEM((8, 128), F32), pltpu.VMEM((shards, 8, 128), F32)]
        + [pltpu.VMEM((8, 128), F32), pltpu.VMEM((nz, 8, 128), F32)]
        + [dma(7), dma(7)] + route_sems + route_sems
        + [dma(shards), dma(shards), dma(nz), dma(nz)]
    )
    hbm = pl.BlockSpec(memory_space=pl.ANY)
    out = pl.pallas_call(
        functools.partial(kernel, nx, ny, nz, entries),
        out_shape=[jax.ShapeDtypeStruct((n, n), BF16)] + [jax.ShapeDtypeStruct((n, n), F32)] * 6,
        in_specs=[hbm, pl.BlockSpec(memory_space=pltpu.SMEM)] + [hbm] * 6,
        out_specs=[hbm] * 7,
        scratch_shapes=scratch,
        compiler_params=pltpu.CompilerParams(
            collective_id=0, has_side_effects=True, vmem_limit_bytes=56 * 1024 * 1024
        ),
        cost_estimate=pl.CostEstimate(flops=62 * 2 * n**3, bytes_accessed=52 * n * n, transcendentals=0),
    )(grads, assignment, *states)
    return (out[0],) + tuple(o[None] for o in out[1:])


def solution(mesh):
    shard_count = mesh.shape["shard"]
    chips = shard_count // 2
    nx = 1
    while nx * nx < chips:
        nx *= 2
    ny = chips // nx
    nz = mesh.shape["tensor"]
    state = P("shard", "tensor", None)

    def run(grads, assignment, *states):
        entries = grads.shape[0] * grads.shape[1]
        program = functools.partial(shards_program, nx, ny, nz, entries)
        return jax.shard_map(
            program,
            mesh=mesh,
            in_specs=(P("shard", "tensor"), P("tensor", None)) + (state,) * 6,
            out_specs=(P("shard", "tensor"),) + (state,) * 6,
            check_vma=False,
        )(grads, assignment, *states)

    return run
```

```python
import functools

import jax
import jax.numpy as jnp
from jax import lax
from jax.experimental import pallas as pl
from jax.experimental.pallas import tpu as pltpu
from jax.sharding import PartitionSpec as P

NS_ITERS = 2
PARTS = 2
LIMIT = 48
BETA_MOMENT = 0.9
BETA_SECOND = 0.9
BETA_STATS = 0.9
ADAM_EPSILON = 1e-08
CLIP_RMS = 1.0
QUINTIC_A = 3.4445
QUINTIC_B = -4.775
QUINTIC_C = 2.0315
MESH = pl.DeviceIdType.MESH
F32 = jnp.float32
BF16 = jnp.bfloat16


def nn(a, b):
    return jnp.dot(a, b, preferred_element_type=F32)


def nt(a, b):
    return lax.dot_general(a, b, (((1,), (1,)), ((), ())), preferred_element_type=F32)


def split(x):
    high = x.astype(BF16)
    return high, (x - high.astype(F32)).astype(BF16)


def put(ref, x, order, axis):
    n = x.shape[0]
    parts = split(x)
    for place, part in enumerate(order):
        if axis:
            ref[:, place * n : (place + 1) * n] = parts[part]
        else:
            ref[place * n : (place + 1) * n, :] = parts[part]


LEFT = (0, 1, 0)
RIGHT = (0, 0, 1)


class Route:
    def __init__(self, nx, ny, rows, src, first, out, second, sems, wanted):
        self.nx, self.ny, self.rows, self.src = nx, ny, rows, src
        self.first, self.out, self.second = first, out, second
        self.send1, self.recv1, self.send2, self.recv2 = sems
        self.wanted = wanted
        me = lax.axis_index("shard")
        self.me = me
        self.core = me % 2
        self.x = (me // 2) % nx
        self.y = me // (2 * nx)
        self.lines = ((nx, self.x, ny, self.y), (ny, self.y, nx, self.x))

    def device(self, kind, along, across, core):
        if kind == 0:
            return {"shard": (across * self.nx + along) * 2 + core}
        return {"shard": (along * self.nx + across) * 2 + core}

    def strip(self, part):
        return slice(part * self.rows, (part + 1) * self.rows)

    def piece(self, kind, part):
        return self.src.at[self.strip(part * 2 + kind), :]

    def copy1(self, kind, part, src, entry, slot, device):
        return pltpu.make_async_remote_copy(
            src_ref=src,
            dst_ref=self.first[kind][part].at[entry],
            send_sem=self.send1.at[kind, part, slot],
            recv_sem=self.recv1.at[kind, part, entry],
            device_id=device,
            device_id_type=MESH,
        )

    def own(self, kind, part, step):
        size, pos, _, other = self.lines[kind]
        device = self.device(kind, (pos + step) % size, other, self.core)
        return self.copy1(kind, part, self.piece(kind, part), pos * 2 + self.core, step, device)

    def relay(self, kind, part, step):
        size, pos, _, other = self.lines[kind]
        entry = ((pos + size - step) % size) * 2 + self.core
        src = self.first[kind][part].at[entry] if step else self.piece(kind, part)
        device = self.device(kind, pos, other, 1 - self.core)
        return self.copy1(kind, part, src, entry, size + step, device)

    def start(self, part):
        for kind in range(2):
            for step in range(1, self.lines[kind][0]):
                self.own(kind, part, step).start()
        for kind in range(2):
            self.relay(kind, part, 0).start()
        for kind in range(2):
            _, pos, _, _ = self.lines[kind]
            self.first[kind][part][pos * 2 + self.core] = self.piece(kind, part)[...]

    def arrived(self, kind, part, entry):
        _, pos, _, other = self.lines[kind]
        device = self.device(kind, pos, other, 1 - self.core)
        self.copy1(kind, part, self.piece(kind, part), entry, 0, device).wait_recv()

    def pass_on(self, part):
        for kind in range(2):
            size, pos, _, _ = self.lines[kind]
            for step in range(1, size):
                self.arrived(kind, part, ((pos + size - step) % size) * 2 + self.core)
                self.relay(kind, part, step).start()

    def copy2(self, kind, part, step, place):
        _, pos, across, other = self.lines[kind]
        return pltpu.make_async_remote_copy(
            src_ref=self.out[kind][part].at[step],
            dst_ref=self.second[kind][part].at[place],
            send_sem=self.send2.at[kind, part, step],
            recv_sem=self.recv2.at[kind, part, place],
            device_id=self.device(kind, pos, (other + step) % across, self.core),
            device_id_type=MESH,
        )

    def entry_of(self, kind, block):
        if kind == 0:
            return block % (2 * self.nx)
        return (block // (2 * self.nx)) * 2 + block % 2

    def choose(self, part):
        for kind in range(2):
            size, pos, across, other = self.lines[kind]
            for step in range(size):
                self.arrived(kind, part, ((pos + size - step) % size) * 2 + 1 - self.core)
            for step in range(1, across):
                to = (other + step) % across
                block = self.wanted(self.device(kind, pos, to, self.core)["shard"])
                self.out[kind][part][step] = self.first[kind][part][self.entry_of(kind, block)]
                self.copy2(kind, part, step, other).start()
            entry = self.entry_of(kind, self.wanted(self.me))
            self.second[kind][part][other] = self.first[kind][part][entry]

    def take(self, part, ref):
        block = self.wanted(self.me)
        for kind in range(2):
            _, _, across, other = self.lines[kind]
            for step in range(1, across):
                self.copy2(kind, part, step, (other + across - step) % across).wait_recv()
            index = block // (2 * self.nx) if kind == 0 else (block // 2) % self.nx
            ref[self.strip(part * 2 + kind), :] = self.second[kind][part][index]

    def finish(self):
        for kind in range(2):
            size, _, across, other = self.lines[kind]
            for part in range(PARTS):
                for step in range(1, size):
                    self.own(kind, part, step).wait_send()
                for step in range(size):
                    self.relay(kind, part, step).wait_send()
                for step in range(1, across):
                    self.copy2(kind, part, step, other).wait_send()


def kernel(nx, ny, nz, entries, *refs):
    (grads, table, moment, second, left, right, pbasis, qbasis) = refs[:8]
    (o_up, o_m, o_v, o_l, o_r, o_p, o_q) = refs[8:15]
    (
        g_v, m_v, v_v, l_v, r_v, p_v, q_v,
        gg, up, mrot, y_s, a_s,
        ptl, plh, qr, qnt, qtl, x1, x2, x3,
        es, ebuf, ezs, ez,
        in_sem, s1, r1, s2, r2, t1, u1, t2, u2, esend, erecv, zsend, zrecv,
    ) = refs[15 : len(refs) - 12 * PARTS]
    buffers = [refs[len(refs) - PARTS * (12 - i) :][:PARTS] for i in range(12)]
    (fx, fy, gx, gy, sx, sy, rfx, rfy, rgx, rgy, rsx, rsy) = buffers
    n = g_v.shape[0]
    half = n // PARTS
    rows = half // 2
    shards = nx * ny * 2
    me = lax.axis_index("shard")
    mz = lax.axis_index("tensor")

    order = ((grads, g_v), (pbasis, p_v), (left, l_v), (moment, m_v), (qbasis, q_v), (second, v_v), (right, r_v))
    loads = [pltpu.make_async_copy(a, b, in_sem.at[i]) for i, (a, b) in enumerate(order)]
    for load in loads:
        load.start()

    barrier = pltpu.get_barrier_semaphore()
    for step in range(1, shards):
        pl.semaphore_signal(barrier, inc=1, device_id={"shard": (me + step) % shards}, device_id_type=MESH)
    for step in range(1, nz):
        pl.semaphore_signal(barrier, inc=1, device_id={"tensor": (mz + step) % nz}, device_id_type=MESH)

    def row_of_slot(device):
        found = jnp.int32(0)
        for k in range(shards):
            found = jnp.where(table[0, k] == device, k, found)
        return found

    used = jnp.bool_(False)
    for k in range(shards):
        used = used | (table[0, k] == me)

    gather = Route(nx, ny, rows, g_v, (fx, fy), (gx, gy), (sx, sy), (s1, r1, s2, r2), row_of_slot)
    give = Route(
        nx, ny, rows, up, (rfx, rfy), (rgx, rgy), (rsx, rsy), (t1, u1, t2, u2), lambda d: table[0, d]
    )

    loads[0].wait()
    pl.semaphore_wait(barrier, shards - 1 + nz - 1)
    for part in range(PARTS):
        gather.start(part)

    gf = g_v[...].astype(F32)
    part = jnp.sum((gf * gf).reshape(n // 8, 8, n), axis=0)
    total = part[:, :128]
    for k in range(1, n // 128):
        total = total + part[:, k * 128 : (k + 1) * 128]
    es[...] = total
    ebuf[me] = total

    def energy_copy(step, src_of):
        return pltpu.make_async_remote_copy(
            src_ref=es,
            dst_ref=ebuf.at[src_of],
            send_sem=esend.at[step],
            recv_sem=erecv.at[src_of],
            device_id={"shard": (me + step) % shards},
            device_id_type=MESH,
        )

    def energy_copy_z(step, src_of):
        return pltpu.make_async_remote_copy(
            src_ref=ezs,
            dst_ref=ez.at[src_of],
            send_sem=zsend.at[step],
            recv_sem=zrecv.at[src_of],
            device_id={"tensor": (mz + step) % nz},
            device_id_type=MESH,
        )

    for step in range(1, shards):
        energy_copy(step, me).start()

    def orth(basis, out, points):
        points[0]()
        y = y_s[...]
        y = y * lax.rsqrt(jnp.sum(y * y) + 1e-12)
        for sweep in range(NS_ITERS):
            y_s[...] = y
            put(x3, y, LEFT, 1)
            put(x2, y, RIGHT, 1)
            put(x1, y, RIGHT, 0)
            points[1 + 3 * sweep]()
            a = nt(x3[...], x2[...])
            a_s[...] = a
            put(x3, a, LEFT, 1)
            put(x2, a, RIGHT, 1)
            points[2 + 3 * sweep]()
            b = nt(x3[...], x2[...])
            put(x3, QUINTIC_B * a_s[...] + QUINTIC_C * b, LEFT, 1)
            points[3 + 3 * sweep]()
            y = QUINTIC_A * y_s[...] + nn(x3[...], x1[...])
        out[...] = jnp.where(used, y.T, basis[...])

    def nothing():
        pass

    loads[1].wait()
    p = p_v[...]
    put(plh, p, LEFT, 1)
    put(ptl, p.T, LEFT, 1)
    loads[2].wait()
    put(x2, l_v[...], RIGHT, 1)
    y_s[...] = nt(ptl[...], x2[...])

    def energy_z():
        for step in range(1, shards):
            energy_copy(step, (me - step) % shards).wait_recv()
        total = jnp.sum(ebuf[...], axis=0)
        ezs[...] = total
        ez[mz] = total
        for step in range(1, nz):
            energy_copy_z(step, mz).start()

    def act(route, name, part):
        return lambda: getattr(route, name)(part)

    orth(
        p_v,
        o_p,
        [
            nothing,
            act(gather, "pass_on", 0),
            act(gather, "choose", 0),
            act(gather, "pass_on", 1),
            act(gather, "choose", 1),
            energy_z,
            nothing,
        ],
    )

    loads[4].wait()
    q = q_v[...]
    put(qr, q, RIGHT, 0)
    put(qnt, q, RIGHT, 1)
    put(qtl, q.T, LEFT, 1)
    loads[3].wait()
    put(x1, m_v[...], RIGHT, 0)
    put(x3, nn(ptl[...], x1[...]), LEFT, 1)
    mrot[...] = nn(x3[...], qr[...])

    for step in range(1, nz):
        energy_copy_z(step, (mz - step) % nz).wait_recv()
    energy = jnp.sum(jnp.sum(ez[...], axis=0), keepdims=True)
    factor = jnp.minimum(1.0, CLIP_RMS / jnp.sqrt(energy / entries + 1e-12))

    for part in range(PARTS):
        gather.take(part, gg)
        g = gg[part * half : (part + 1) * half, :]
        high = nn(ptl[:, part * half : (part + 1) * half], g)
        term = high + nn(ptl[:, n + part * half : n + (part + 1) * half], g)
        a_s[...] = term if part == 0 else a_s[...] + term
    put(x3, a_s[...], LEFT, 1)
    rotated = factor * nn(x3[...], qr[...])
    loads[5].wait()
    v_new = BETA_SECOND * v_v[...] + (1.0 - BETA_SECOND) * rotated * rotated
    direction = (BETA_MOMENT * mrot[...] + (1.0 - BETA_MOMENT) * rotated) / (jnp.sqrt(v_new) + ADAM_EPSILON)
    o_v[...] = jnp.where(used, v_new, v_v[...])
    put(x1, direction, RIGHT, 0)
    for part in range(PARTS):
        strip = slice(part * half, (part + 1) * half)
        high, low = split(nn(plh[strip, :], x1[...]))
        x3[strip, 0:n] = high
        x3[strip, n : 2 * n] = low
        x3[strip, 2 * n : 3 * n] = high
        up[strip, :] = nt(x3[strip, :], qnt[...]).astype(BF16)
        give.start(part)

    keep_m = jnp.where(used, BETA_MOMENT, 1.0)
    add_m = jnp.where(used, (1.0 - BETA_MOMENT) * factor, 0.0)
    keep_s = jnp.where(used, BETA_STATS, 1.0)
    add_s = jnp.where(used, (1.0 - BETA_STATS) * factor * factor / n, 0.0)
    o_m[...] = keep_m * m_v[...] + add_m * gg[...].astype(F32)
    loads[6].wait()
    put(x2, r_v[...], RIGHT, 1)
    y_s[...] = nt(qtl[...], x2[...])
    g = gg[...]
    o_l[...] = keep_s * l_v[...] + add_s * nt(g, g)
    gt = g.T
    o_r[...] = keep_s * r_v[...] + add_s * nt(gt, gt)

    orth(
        q_v,
        o_q,
        [
            act(give, "pass_on", 0),
            act(give, "choose", 0),
            act(give, "pass_on", 1),
            act(give, "choose", 1),
            nothing,
            nothing,
            nothing,
        ],
    )

    gather.finish()
    for step in range(1, shards):
        energy_copy(step, me).wait_send()
    for step in range(1, nz):
        energy_copy_z(step, mz).wait_send()
    for part in range(PARTS):
        give.take(part, o_up)
    give.finish()


def hand_on(*refs):
    sems = refs[14]
    copies = [pltpu.make_async_copy(refs[i], refs[7 + i], sems.at[i]) for i in range(7)]
    for copy in copies:
        copy.start()
    for copy in copies:
        copy.wait()


def shards_program(nx, ny, nz, entries, grads, assignment, *states):
    n = grads.shape[1]
    half = n // 2
    states = [s.reshape(n, n) for s in states]
    square = lambda dtype: pltpu.VMEM((n, n), dtype)
    wide = pltpu.VMEM((n, 3 * n), BF16)
    tall = pltpu.VMEM((3 * n, n), BF16)
    pieces = lambda count: [pltpu.VMEM((count, half // PARTS, n), BF16)] * PARTS
    longest = max(nx, ny)
    dma = lambda *shape: pltpu.SemaphoreType.DMA(shape)
    route = sum((pieces(count) for count in (2 * nx, 2 * ny, ny, nx, ny, nx)), [])
    route_sems = [dma(2, PARTS, 2 * longest)] * 2 + [dma(2, PARTS, longest)] * 2
    shards = nx * ny * 2
    scratch = (
        [square(BF16)] + [square(F32)] * 6
        + [square(BF16), square(BF16), square(F32), square(F32), square(F32)]
        + [wide, wide, tall, wide, wide, tall, wide, wide]
        + [pltpu.VMEM((8, 128), F32), pltpu.VMEM((shards, 8, 128), F32)]
        + [pltpu.VMEM((8, 128), F32), pltpu.VMEM((nz, 8, 128), F32)]
        + [dma(7)] + route_sems + route_sems
        + [dma(shards), dma(shards), dma(nz), dma(nz)]
        + route + route
    )
    vmem = pl.BlockSpec(memory_space=pltpu.VMEM)
    hbm = pl.BlockSpec(memory_space=pl.ANY)
    out = pl.pallas_call(
        functools.partial(kernel, nx, ny, nz, entries),
        out_shape=[square(BF16)] + [square(F32)] * 6,
        in_specs=[hbm, pl.BlockSpec(memory_space=pltpu.SMEM)] + [hbm] * 6,
        out_specs=[vmem] * 7,
        scratch_shapes=scratch,
        compiler_params=pltpu.CompilerParams(
            collective_id=0, has_side_effects=True, vmem_limit_bytes=LIMIT * 1024 * 1024
        ),
        cost_estimate=pl.CostEstimate(flops=62 * 2 * n**3, bytes_accessed=52 * n * n, transcendentals=0),
    )(grads, assignment, *states)
    out = pl.pallas_call(
        hand_on,
        out_shape=[jax.ShapeDtypeStruct(o.shape, o.dtype) for o in out],
        in_specs=[hbm] * 7,
        out_specs=[hbm] * 7,
        scratch_shapes=[dma(7)],
        compiler_params=pltpu.CompilerParams(vmem_limit_bytes=1024 * 1024),
        cost_estimate=pl.CostEstimate(flops=0, bytes_accessed=52 * n * n, transcendentals=0),
    )(*out)
    return (out[0],) + tuple(o[None] for o in out[1:])


def solution(mesh):
    shard_count = mesh.shape["shard"]
    chips = shard_count // 2
    nx = 1
    while nx * nx < chips:
        nx *= 2
    ny = chips // nx
    nz = mesh.shape["tensor"]
    state = P("shard", "tensor", None)

    def run(grads, assignment, *states):
        entries = grads.shape[0] * grads.shape[1]
        program = functools.partial(shards_program, nx, ny, nz, entries)
        return jax.shard_map(
            program,
            mesh=mesh,
            in_specs=(P("shard", "tensor"), P("tensor", None)) + (state,) * 6,
            out_specs=(P("shard", "tensor"),) + (state,) * 6,
            check_vma=False,
        )(grads, assignment, *states)

    return run
```
